256 devices in a mesh: chan: 128 (over z_lo, x, y, core), day: 2 (over z_hi).
Axes of the slice: x: 4, y: 4, z: 8 (z_hi: 2, z_lo: 4; z = z_hi * 4 + z_lo), core: 2. Of those that a mesh axis runs over, the one named last changes fastest.
Arguments:
- spectra: bfloat16 [4096, 64, 400], P('chan', 'day'), may hold values from -6 to 6
- owners: int32 [2], replicated, may hold values from 0 to 127
Outputs:
- stacks: bfloat16 [2, 4096, 32, 400], P(None, ('chan', 'day'))
The draws below stay inside these ranges and needn't reach their ends.
Inputs may be any that keep to these rules, and one draw needn't show every extreme that they name: `owners`: block indices along the channel axis; two steps may name the same block.
All inputs are finite; a program needn't handle non-finite values.
Results may differ from the reference program's by a relative error of at most 0.0073.
Values may be sent and summed in bfloat16 or wider, within the bound.
No kernel may reach another device: no remote copies, remote signals or barrier semaphores. Data moves between devices by JAX's collectives and lax.ppermute only.
A program may use at most 64 MiB of HBM per device.

```python
import math
import jax
import jax.numpy as jnp
from jax import lax

F = 200
LAGS = 400
CH_DEV = 32
WIN_DEV = 32
STEPS = 2
CHANNELS = 4096
WINDOWS = 64
N_CHAN = 128
N_DAY = 2


def block_scale(key, dims, split, smallest, largest):
    level = 1.0
    for axis_at, parts in split:
        steps = jax.random.uniform(jax.random.fold_in(jax.random.fold_in(key, 6), axis_at), (parts,), jnp.float32, smallest / len(split), largest / len(split))
        level = level * jnp.repeat(jnp.exp(steps), dims[axis_at] // parts).reshape((-1,) + (1,) * (len(dims) - 1 - axis_at))
    return level


def centred(own_key, extent, deviation, limit, cuts=(), held_as=jnp.bfloat16):
    result = deviation * jax.random.normal(own_key, extent, jnp.float32)
    if cuts:
        result = result * block_scale(own_key, extent, cuts, -0.22, 0.18)
    return jnp.clip(result, -limit, limit).astype(held_as)


def setup_inputs(seed: int = 0) -> dict:
    keys = jax.random.split(jax.random.key(seed), 3)
    return {
        "spectra": centred(keys[0], (CHANNELS, WINDOWS, 2 * F), 1.0, 6.0, ((0, 128), (1, 2))),
        "owners": jax.random.randint(keys[1], (STEPS,), 0, N_CHAN).astype(jnp.int32),
    }


def whiten(spectra, bins):
    values = spectra.astype(jnp.float32)
    real_part = values[..., :bins]
    imag_part = values[..., bins:]
    power = real_part * real_part + imag_part * imag_part
    mean_power = lax.optimization_barrier(jnp.mean(power, axis=-1, keepdims=True))
    factor = lax.rsqrt(power + 0.25 * mean_power + 1e-06)
    return jnp.concatenate([real_part * factor, imag_part * factor], axis=-1).astype(jnp.bfloat16)

def lag_table(bins, lag_count):
    freqs = jnp.arange(bins, dtype=jnp.int32)
    shifts = jnp.arange(lag_count, dtype=jnp.int32) - lag_count // 2
    phase = jnp.mod(freqs[:, None] * shifts[None, :], 2 * bins)
    angle = phase.astype(jnp.float32) * (math.pi / bins)
    return jnp.concatenate([jnp.cos(angle), -jnp.sin(angle)], axis=0).astype(jnp.bfloat16)

def day_cross(own, other, bins):
    own_f = own.astype(jnp.float32)
    other_f = other.astype(jnp.float32)
    own_re, own_im = (own_f[..., :bins], own_f[..., bins:])
    oth_re, oth_im = (other_f[..., :bins], other_f[..., bins:])
    cross_re = jnp.einsum('iwf,jwf->ijf', own_re, oth_re) + jnp.einsum('iwf,jwf->ijf', own_im, oth_im)
    cross_im = jnp.einsum('iwf,jwf->ijf', own_im, oth_re) - jnp.einsum('iwf,jwf->ijf', own_re, oth_im)
    return jnp.concatenate([cross_re, cross_im], axis=-1).astype(jnp.bfloat16)

def reference(spectra, owners):
    white = whiten(spectra, F)
    table = lag_table(F, LAGS)
    norm = 1.0 / math.sqrt(WINDOWS * F)
    groups = white.reshape(N_CHAN, CH_DEV, WINDOWS, 2 * F)
    results = []
    for step in range(STEPS):
        start = (owners[step] * CH_DEV).astype(jnp.int32)
        block = lax.dynamic_slice_in_dim(white, start, CH_DEV, 0)

        def one_group(own):
            total = jnp.zeros((CH_DEV, CH_DEV, 2 * F), jnp.float32)
            for day in range(N_DAY):
                lo = day * WIN_DEV
                part = day_cross(own[:, lo:lo + WIN_DEV], block[:, lo:lo + WIN_DEV], F)
                total = total + part.astype(jnp.float32)
            summed = total.astype(jnp.bfloat16).reshape(CH_DEV * CH_DEV, 2 * F)
            lagged = jnp.dot(summed, table, preferred_element_type=jnp.float32) * norm
            return lagged.reshape(CH_DEV, CH_DEV, LAGS).astype(jnp.bfloat16)
        stacked = lax.map(one_group, groups)
        results.append(stacked.reshape(CHANNELS, CH_DEV, LAGS))
    return jnp.stack(results, axis=0)
```

```python
import math

import jax
import jax.numpy as jnp
from jax import lax
from jax.sharding import Mesh, PartitionSpec as P

LAGS = 400
STEPS = 2
BINS = 200
SHARE = 7
PLANE = ("x", "y", "core")
SIDE = 32
ALL = ("z", "x", "y", "core")


def whiten(spectra):
    values = spectra.astype(jnp.float32)
    real_part = values[..., :BINS]
    imag_part = values[..., BINS:]
    power = real_part * real_part + imag_part * imag_part
    mean_power = jnp.mean(power, axis=-1, keepdims=True)
    factor = lax.rsqrt(power + 0.25 * mean_power + 1e-06)
    return jnp.stack([real_part * factor, imag_part * factor], axis=-2).astype(jnp.bfloat16)


def lag_table():
    freqs = jnp.arange(BINS, dtype=jnp.int32)
    shifts = jnp.arange(LAGS, dtype=jnp.int32) - LAGS // 2
    phase = jnp.mod(freqs[:, None] * shifts[None, :], 2 * BINS)
    angle = phase.astype(jnp.float32) * (math.pi / BINS)
    return jnp.stack([jnp.cos(angle), -jnp.sin(angle)], axis=0).astype(jnp.bfloat16)


def by_bins(white):
    rows, wins = white.shape[:2]
    padded = jnp.pad(white, ((0, 0), (0, 0), (0, 0), (0, SIDE * SHARE - BINS)))
    return padded.reshape(rows, wins, 2, SIDE, SHARE).transpose(3, 4, 2, 0, 1)


def ring(shift):
    at = [(r % 4) * 2 + r // 4 for r in range(8)]
    return [(at[r], at[(r + shift) % 8]) for r in range(8)]


def hop(array, shift):
    return lax.ppermute(array, ("z", "day"), ring(shift))


def spread(array):
    rows, width = array.shape[0], array[0].size
    flat = array.reshape(rows, width // 128, 128)
    return lax.all_to_all(flat, PLANE, 0, 0, tiled=True).reshape(array.shape)


def local(spectra, owners):
    day = lax.axis_index("day")
    z_lo = lax.axis_index("z")
    half = spectra.shape[0] // 2
    theirs = lax.dynamic_slice_in_dim(spectra, (1 - day) * half, half, 0)
    other_raw = lax.ppermute(theirs.reshape(-1, 128), "day", [(0, 1), (1, 0)]).reshape(theirs.shape)

    own = spread(by_bins(whiten(spectra)))
    pieces = []
    for step in range(STEPS):
        piece = lax.dynamic_index_in_dim(own, owners[step] % SIDE, 0, keepdims=False)
        pieces.append(jnp.where(owners[step] // SIDE == z_lo, piece, jnp.zeros_like(piece)))
    held = jnp.stack(pieces)
    shape = held.shape
    held = held.reshape(STEPS, -1, 128)
    near = held + hop(held, 1) + hop(held, -1)
    below, above = hop(near, 3), hop(near, -3)
    ring_at = day * 4 + z_lo
    blocks = []
    for which in range(2):
        chosen = []
        for step in range(STEPS):
            home = owners[step] // SIDE + 4 * which
            delta = jnp.mod(ring_at - home + 16, 8)
            chosen.append(
                jnp.where(
                    (delta == 7) | (delta <= 1),
                    near[step],
                    jnp.where(delta <= 4, below[step], above[step]),
                )
            )
        blocks.append(jnp.stack(chosen))
    mine = jnp.where(day == 0, blocks[0], blocks[1]).reshape(shape)
    other = jnp.where(day == 0, blocks[1], blocks[0]).reshape(shape)

    other_rows = spread(by_bins(whiten(other_raw)))
    own_rows = lax.dynamic_slice_in_dim(own, day * half, half, 3)
    left = jnp.concatenate([own_rows, other_rows], axis=-1)
    right = jnp.concatenate([mine, other], axis=-1)
    product = jnp.einsum("akpiw,skcjw->kaipcsj", left, right, preferred_element_type=jnp.float32)
    real_part = product[:, :, :, 0, 0] + product[:, :, :, 1, 1]
    imag_part = product[:, :, :, 1, 0] - product[:, :, :, 0, 1]
    cross = jnp.stack([real_part, imag_part], axis=3).astype(jnp.bfloat16)
    home_rows = spread(cross.transpose(1, 0, 2, 3, 4, 5))
    summed = home_rows.reshape((SIDE * SHARE,) + home_rows.shape[2:])[:BINS]
    norm = 1.0 / math.sqrt(2 * spectra.shape[1] * BINS)
    lagged = jnp.einsum("ficsj,cfl->sijl", summed, lag_table(), preferred_element_type=jnp.float32)
    return (lagged * norm).astype(jnp.bfloat16)


def solution(mesh):
    fine = Mesh(mesh.devices.reshape(4, 4, 4, 2, 2), ALL + ("day",))
    return jax.shard_map(
        local,
        mesh=fine,
        in_specs=(P(ALL, "day", None), P()),
        out_specs=P(None, ALL + ("day",), None, None),
        check_vma=False,
    )
```

```python
import math

import jax
import jax.numpy as jnp
from jax import lax
from jax.experimental import pallas as pl
from jax.experimental.pallas import tpu as pltpu
from jax.sharding import Mesh, PartitionSpec as P

LAGS = 400
STEPS = 2
BINS = 200
SHARE = 7
SIDE = 32
PLANE = ("x", "y", "core")
ALL = ("z", "x", "y", "core")
ROWS = SHARE * 16
HALF = SHARE * 8
VMEM = pl.BlockSpec(memory_space=pltpu.VMEM)
SMEM = pl.BlockSpec(memory_space=pltpu.SMEM)
ROOM = pltpu.CompilerParams(vmem_limit_bytes=48 * 1024 * 1024)


def lag_table():
    freqs = jnp.arange(BINS, dtype=jnp.int32)
    shifts = jnp.arange(LAGS, dtype=jnp.int32) - LAGS // 2
    phase = jnp.mod(freqs[:, None] * shifts[None, :], 2 * BINS)
    angle = phase.astype(jnp.float32) * (math.pi / BINS)
    return jnp.stack([jnp.cos(angle), -jnp.sin(angle)], axis=0).astype(jnp.bfloat16)


def prep_kernel(place_ref, spectra_ref, out_ref, theirs_ref, rows_ref):
    day = place_ref[0]
    low = lax.broadcasted_iota(jnp.int32, (BINS, 128), 1) < 64
    pad = SIDE * SHARE - BINS
    rows_ref[BINS * 16 :, :] = jnp.zeros((pad * 16, 128), jnp.float32)
    for half in range(2):
        for pair in range(4):
            parts = []
            for a in (2 * pair, 2 * pair + 1):
                for q in range(2):
                    parts.append(spectra_ref[half * 16 + q * 8 + a].astype(jnp.float32))
            turned = jnp.concatenate(parts, axis=0).T
            re, im = turned[:BINS], turned[BINS:]
            power = re * re + im * im
            mean_power = jnp.mean(power, axis=0, keepdims=True)
            factor = lax.rsqrt(power + 0.25 * mean_power + 1e-06)
            re, im = re * factor, im * factor
            first = jnp.where(low, re, pltpu.roll(im, 64, 1))
            second = jnp.where(low, pltpu.roll(re, 64, 1), im)
            at = half * 8 + 2 * pair
            rows_ref[pl.ds(at, BINS, stride=16), :] = first
            rows_ref[pl.ds(at + 1, BINS, stride=16), :] = second
    for dest in range(SIDE):
        chunk = rows_ref[dest * ROWS : (dest + 1) * ROWS, :]
        out_ref[dest] = chunk.astype(jnp.bfloat16)
        split = chunk.reshape(SHARE, 2, 8, 128)
        theirs = jnp.where(day == 0, split[:, 1], split[:, 0])
        theirs_ref[dest] = theirs.reshape(HALF, 128).astype(jnp.bfloat16)


def prep(place, spectra):
    return pl.pallas_call(
        prep_kernel,
        out_shape=(
            jax.ShapeDtypeStruct((SIDE, ROWS, 128), jnp.bfloat16),
            jax.ShapeDtypeStruct((SIDE, HALF, 128), jnp.bfloat16),
        ),
        in_specs=[SMEM, VMEM],
        out_specs=(VMEM, VMEM),
        scratch_shapes=[pltpu.VMEM((SIDE * ROWS, 128), jnp.float32)],
        compiler_params=ROOM,
        name="prep",
    )(place, spectra)


def weights(value):
    lane = lax.broadcasted_iota(jnp.int32, value.shape, 1)
    odd = (lane // 32) % 2 == 1
    zero = jnp.zeros_like(value)
    even_v, odd_v = jnp.where(odd, zero, value), jnp.where(odd, value, zero)
    at = ((even_v, pltpu.roll(odd_v, 96, 1)), (pltpu.roll(even_v, 32, 1), odd_v))
    rows = []
    for q_i in range(2):
        for c in range(2):
            parts = []
            for q_j in range(2):
                part = at[q_i][q_j]
                if c == 1:
                    part = pltpu.roll(part, 64, 1)
                    part = jnp.where(lane < 64, -part, part)
                parts.append(part)
            rows.append(
                jnp.concatenate([parts[0][:8], parts[1][:8], parts[0][8:], parts[1][8:]], axis=0)
            )
    return rows


def cross_kernel(place_ref, own_ref, other_ref, near_ref, below_ref, above_ref, out_ref):
    day, z_lo = place_ref[0], place_ref[1]
    blocks = []
    for which in range(2):
        day_of = (day + which) % 2
        chosen = []
        for step in range(STEPS):
            home = place_ref[2 + step] // SIDE + 4 * day_of
            delta = (day * 4 + z_lo - home + 16) % 8
            use_near = (delta == 7) | (delta <= 1)
            use_below = delta <= 4
            near = near_ref[step].astype(jnp.float32)
            below = below_ref[step].astype(jnp.float32)
            above = above_ref[step].astype(jnp.float32)
            chosen.append(jnp.where(use_near, near, jnp.where(use_below, below, above)))
        blocks.append(chosen)
    own_all = own_ref[...].astype(jnp.float32).reshape(SIDE, SHARE, 2, 8, 128)
    other_all = other_ref[...].astype(jnp.float32).reshape(SIDE, SHARE, 8, 128)
    for k in range(SHARE):
        sides = []
        for which in range(2):
            parts = [weights(blocks[which][step][k * 16 : k * 16 + 16]) for step in range(STEPS)]
            order = []
            for at in range(4):
                for step in range(STEPS):
                    order.append(parts[step][at])
            sides.append(jnp.concatenate(order, axis=0))
        right = jnp.concatenate(sides, axis=1).astype(jnp.bfloat16)
        own = jnp.where(day == 0, own_all[:, k, 0], own_all[:, k, 1]).reshape(SIDE * 8, 128)
        other = other_all[:, k].reshape(SIDE * 8, 128)
        left = jnp.concatenate([own, other], axis=1).astype(jnp.bfloat16)
        product = lax.dot_general(
            left, right, (((1,), (1,)), ((), ())), preferred_element_type=jnp.float32
        )
        low = product[:, :128].reshape(SIDE, 8, 128)
        high = product[:, 128:].reshape(SIDE, 8, 128)
        both = jnp.concatenate([low, high], axis=1)
        out_ref[:, k * 16 : k * 16 + 16, :] = both.astype(jnp.bfloat16)


def cross(place, own, other, near, below, above):
    return pl.pallas_call(
        cross_kernel,
        out_shape=jax.ShapeDtypeStruct((SIDE, ROWS, 128), jnp.bfloat16),
        in_specs=[SMEM] + [VMEM] * 5,
        out_specs=VMEM,
        compiler_params=ROOM,
        name="cross",
    )(place, own, other, near, below, above)


def lag_kernel(norm, summed_ref, table_ref, out_ref, rows_ref):
    rows_ref[...] = summed_ref[...].astype(jnp.float32).reshape(SIDE * ROWS, 128)
    for i in range(16):
        turned = rows_ref[pl.ds(i, BINS, stride=16), :].T.astype(jnp.bfloat16)
        lagged = jnp.dot(turned[:64], table_ref[0], preferred_element_type=jnp.float32)
        lagged = lagged + jnp.dot(turned[64:], table_ref[1], preferred_element_type=jnp.float32)
        lagged = (lagged * norm).astype(jnp.bfloat16)
        for step in range(STEPS):
            out_ref[step, i] = lagged[step * 32 : step * 32 + 32]


def lag(norm, summed, table):
    def kernel(*refs):
        lag_kernel(norm, *refs)

    return pl.pallas_call(
        kernel,
        out_shape=jax.ShapeDtypeStruct((STEPS, 16, 32, LAGS), jnp.bfloat16),
        in_specs=[VMEM, VMEM],
        out_specs=VMEM,
        scratch_shapes=[pltpu.VMEM((SIDE * ROWS, 128), jnp.float32)],
        compiler_params=ROOM,
        name="lag",
    )(summed, table)


def hop(array, shift):
    at = [(r % 4) * 2 + r // 4 for r in range(8)]
    ring = [(at[r], at[(r + shift) % 8]) for r in range(8)]
    return lax.ppermute(array, ("z", "day"), ring)


def spread(array):
    return lax.all_to_all(array, PLANE, 0, 0, tiled=True)


def local(spectra, owners):
    day = lax.axis_index("day").astype(jnp.int32)
    z_lo = lax.axis_index("z").astype(jnp.int32)
    place = jnp.concatenate([jnp.stack([day, z_lo]), owners])
    mine, theirs = prep(place, spectra)
    arrived = lax.ppermute(theirs, "day", [(0, 1), (1, 0)])
    own = spread(mine)
    pieces = []
    for step in range(STEPS):
        piece = lax.dynamic_index_in_dim(own, owners[step] % SIDE, 0, keepdims=False)
        pieces.append(jnp.where(owners[step] // SIDE == z_lo, piece, jnp.zeros_like(piece)))
    held = jnp.stack(pieces)
    near = held + hop(held, 1) + hop(held, -1)
    below, above = hop(near, 3), hop(near, -3)
    other = spread(arrived)
    home = spread(cross(place, own, other, near, below, above))
    norm = 1.0 / math.sqrt(2 * spectra.shape[1] * BINS)
    return lag(norm, home, lag_table())


def solution(mesh):
    fine = Mesh(mesh.devices.reshape(4, 4, 4, 2, 2), ALL + ("day",))
    return jax.shard_map(
        local,
        mesh=fine,
        in_specs=(P(ALL, "day", None), P()),
        out_specs=P(None, ALL + ("day",), None, None),
        check_vma=False,
    )
```

```python
import math

import jax
import jax.numpy as jnp
from jax import lax
from jax.experimental import pallas as pl
from jax.experimental.pallas import tpu as pltpu
from jax.sharding import Mesh, PartitionSpec as P

LAGS = 400
STEPS = 2
BINS = 200
SHARE = 7
SIDE = 32
PLANE = ("x", "y", "core")
ALL = ("z", "x", "y", "core")
ROWS = SHARE * 16
HALF = SHARE * 8
VMEM = pl.BlockSpec(memory_space=pltpu.VMEM)
SMEM = pl.BlockSpec(memory_space=pltpu.SMEM)
ROOM = pltpu.CompilerParams(vmem_limit_bytes=48 * 1024 * 1024)


def lag_table():
    freqs = jnp.arange(BINS, dtype=jnp.int32)
    shifts = jnp.arange(LAGS, dtype=jnp.int32) - LAGS // 2
    phase = jnp.mod(freqs[:, None] * shifts[None, :], 2 * BINS)
    angle = phase.astype(jnp.float32) * (math.pi / BINS)
    return jnp.stack([jnp.cos(angle), -jnp.sin(angle)], axis=0).astype(jnp.bfloat16)


def prep_kernel(spectra_ref, out_ref, theirs_ref, held_ref, sems, rows_ref):
    day = lax.axis_index("day")
    copies = []
    for which in range(2):
        half = (day + which) % 2
        copies.append(
            pltpu.make_async_copy(
                spectra_ref.at[pl.ds(half * 16, 16)],
                held_ref.at[pl.ds(which * 16, 16)],
                sems.at[which],
            )
        )
    for copy in copies:
        copy.start()
    low = lax.broadcasted_iota(jnp.int32, (BINS, 128), 1) < 64
    rows_ref[BINS * 16 :, :] = jnp.zeros(((SIDE * SHARE - BINS) * 16, 128), jnp.float32)
    for which in range(2):
        copies[which].wait()
        for pair in range(4):
            parts = []
            for a in (2 * pair, 2 * pair + 1):
                for q in range(2):
                    parts.append(held_ref[which * 16 + q * 8 + a].astype(jnp.float32))
            turned = jnp.concatenate(parts, axis=0).T
            re, im = turned[:BINS], turned[BINS:]
            power = re * re + im * im
            mean_power = jnp.mean(power, axis=0, keepdims=True)
            factor = lax.rsqrt(power + 0.25 * mean_power + 1e-06)
            re, im = re * factor, im * factor
            first = jnp.where(low, re, pltpu.roll(im, 64, 1))
            second = jnp.where(low, pltpu.roll(re, 64, 1), im)
            at = which * 8 + 2 * pair
            rows_ref[pl.ds(at, BINS, stride=16), :] = first
            rows_ref[pl.ds(at + 1, BINS, stride=16), :] = second
    for dest in range(SIDE):
        chunk = rows_ref[dest * ROWS : (dest + 1) * ROWS, :]
        out_ref[dest] = chunk.astype(jnp.bfloat16)
        theirs = chunk.reshape(SHARE, 2, 8, 128)[:, 1].reshape(HALF, 128)
        count = min(HALF, BINS * 8 - dest * HALF)
        if count > 0:
            theirs_ref[dest * HALF : dest * HALF + count, :] = theirs[:count].astype(jnp.bfloat16)


def prep(spectra):
    return pl.pallas_call(
        prep_kernel,
        out_shape=(
            jax.ShapeDtypeStruct((SIDE, ROWS, 128), jnp.bfloat16),
            jax.ShapeDtypeStruct((BINS * 8, 128), jnp.bfloat16),
        ),
        in_specs=[pl.BlockSpec(memory_space=pl.ANY)],
        out_specs=(VMEM, VMEM),
        scratch_shapes=[
            pltpu.VMEM(spectra.shape, jnp.bfloat16),
            pltpu.SemaphoreType.DMA((2,)),
            pltpu.VMEM((SIDE * ROWS, 128), jnp.float32),
        ],
        compiler_params=pltpu.CompilerParams(vmem_limit_bytes=60 * 1024 * 1024),
        name="prep",
    )(spectra)


def weights(value, day_of):
    swapped = jnp.concatenate([value[8:], value[:8]], axis=0)
    value = jnp.where(day_of == 0, value, swapped)
    lane = lax.broadcasted_iota(jnp.int32, value.shape, 1)
    odd = (lane // 32) % 2 == 1
    zero = jnp.zeros_like(value)
    even_v, odd_v = jnp.where(odd, zero, value), jnp.where(odd, value, zero)
    at = ((even_v, pltpu.roll(odd_v, 96, 1)), (pltpu.roll(even_v, 32, 1), odd_v))
    rows = []
    for q_i in range(2):
        for c in range(2):
            parts = []
            for q_j in range(2):
                part = at[q_i][q_j]
                if c == 1:
                    part = pltpu.roll(part, 64, 1)
                    part = jnp.where(lane < 64, -part, part)
                parts.append(part)
            rows.append(
                jnp.concatenate([parts[0][:8], parts[1][:8], parts[0][8:], parts[1][8:]], axis=0)
            )
    return rows


def cross_kernel(owners_ref, own_ref, other_ref, near_ref, below_ref, above_ref, out_ref):
    day, z_lo = lax.axis_index("day"), lax.axis_index("z")
    blocks = []
    for which in range(2):
        day_of = (day + which) % 2
        chosen = []
        for step in range(STEPS):
            home = owners_ref[step] // SIDE + 4 * day_of
            delta = (day * 4 + z_lo - home + 16) % 8
            use_near = (delta == 7) | (delta <= 1)
            use_below = delta <= 4
            near = near_ref[step].astype(jnp.float32)
            below = below_ref[step].astype(jnp.float32)
            above = above_ref[step].astype(jnp.float32)
            chosen.append(jnp.where(use_near, near, jnp.where(use_below, below, above)))
        blocks.append(chosen)
    own_all = own_ref[...].astype(jnp.float32).reshape(SIDE, SHARE, 2, 8, 128)
    other_all = other_ref[...].astype(jnp.float32).reshape(SIDE, SHARE, 8, 128)
    for k in range(SHARE):
        sides = []
        for which in range(2):
            day_of = (day + which) % 2
            parts = [
                weights(blocks[which][step][k * 16 : k * 16 + 16], day_of) for step in range(STEPS)
            ]
            order = []
            for at in range(4):
                for step in range(STEPS):
                    order.append(parts[step][at])
            sides.append(jnp.concatenate(order, axis=0))
        right = jnp.concatenate(sides, axis=1).astype(jnp.bfloat16)
        own = own_all[:, k, 0].reshape(SIDE * 8, 128)
        other = other_all[:, k].reshape(SIDE * 8, 128)
        left = jnp.concatenate([own, other], axis=1).astype(jnp.bfloat16)
        product = lax.dot_general(
            left, right, (((1,), (1,)), ((), ())), preferred_element_type=jnp.float32
        )
        low = product[:, :128].reshape(SIDE, 8, 128)
        high = product[:, 128:].reshape(SIDE, 8, 128)
        both = jnp.concatenate([low, high], axis=1)
        out_ref[:, k * 16 : k * 16 + 16, :] = both.astype(jnp.bfloat16)


def cross(owners, own, other, near, below, above):
    return pl.pallas_call(
        cross_kernel,
        out_shape=jax.ShapeDtypeStruct((SIDE, ROWS, 128), jnp.bfloat16),
        in_specs=[SMEM] + [VMEM] * 5,
        out_specs=VMEM,
        compiler_params=ROOM,
        name="cross",
    )(owners, own, other, near, below, above)


def lag_kernel(norm, summed_ref, table_ref, out_ref, rows_ref):
    rows_ref[...] = summed_ref[...].astype(jnp.float32).reshape(SIDE * ROWS, 128)
    for i in range(16):
        turned = rows_ref[pl.ds(i, BINS, stride=16), :].T.astype(jnp.bfloat16)
        lagged = jnp.dot(turned[:64], table_ref[0], preferred_element_type=jnp.float32)
        lagged = lagged + jnp.dot(turned[64:], table_ref[1], preferred_element_type=jnp.float32)
        lagged = (lagged * norm).astype(jnp.bfloat16)
        for step in range(STEPS):
            out_ref[step, i] = lagged[step * 32 : step * 32 + 32]


def lag(norm, summed, table):
    def kernel(*refs):
        lag_kernel(norm, *refs)

    return pl.pallas_call(
        kernel,
        out_shape=jax.ShapeDtypeStruct((STEPS, 16, 32, LAGS), jnp.bfloat16),
        in_specs=[VMEM, VMEM],
        out_specs=VMEM,
        scratch_shapes=[pltpu.VMEM((SIDE * ROWS, 128), jnp.float32)],
        compiler_params=ROOM,
        name="lag",
    )(summed, table)


def hop(array, shift):
    at = [(r % 4) * 2 + r // 4 for r in range(8)]
    ring = [(at[r], at[(r + shift) % 8]) for r in range(8)]
    return lax.ppermute(array, ("z", "day"), ring)


def spread(array):
    return lax.all_to_all(array, PLANE, 0, 0, tiled=True)


def local(spectra, owners):
    z_lo = lax.axis_index("z")
    mine, theirs = prep(spectra)
    arrived = lax.ppermute(theirs, "day", [(0, 1), (1, 0)])
    own = spread(mine)
    pieces = []
    for step in range(STEPS):
        piece = lax.dynamic_index_in_dim(own, owners[step] % SIDE, 0, keepdims=False)
        pieces.append(jnp.where(owners[step] // SIDE == z_lo, piece, jnp.zeros_like(piece)))
    held = jnp.stack(pieces)
    near = held + hop(held, 1) + hop(held, -1)
    below, above = hop(near, 3), hop(near, -3)
    arrived = jnp.pad(arrived, ((0, SIDE * HALF - BINS * 8), (0, 0))).reshape(SIDE, HALF, 128)
    arrived, near = lax.optimization_barrier((arrived, near))
    other = spread(arrived)
    home = spread(cross(owners, own, other, near, below, above))
    norm = 1.0 / math.sqrt(2 * spectra.shape[1] * BINS)
    return lag(norm, home, lag_table())


def solution(mesh):
    fine = Mesh(mesh.devices.reshape(4, 4, 4, 2, 2), ALL + ("day",))
    return jax.shard_map(
        local,
        mesh=fine,
        in_specs=(P(ALL, "day", None), P()),
        out_specs=P(None, ALL + ("day",), None, None),
        check_vma=False,
    )
```

```python
import math

import jax
import jax.numpy as jnp
from jax import lax
from jax.experimental import pallas as pl
from jax.experimental.pallas import tpu as pltpu
from jax.sharding import Mesh, PartitionSpec as P

LAGS = 400
STEPS = 2
BINS = 200
SHARE = 7
SIDE = 32
PLANE = ("x", "y", "core")
ALL = ("z", "x", "y", "core")
ROWS = SHARE * 16
HALF = SHARE * 8
VMEM = pl.BlockSpec(memory_space=pltpu.VMEM)
ROOM = pltpu.CompilerParams(vmem_limit_bytes=48 * 1024 * 1024)


def lag_table():
    freqs = jnp.arange(BINS, dtype=jnp.int32)
    shifts = jnp.arange(LAGS, dtype=jnp.int32) - LAGS // 2
    phase = jnp.mod(freqs[:, None] * shifts[None, :], 2 * BINS)
    angle = phase.astype(jnp.float32) * (math.pi / BINS)
    return jnp.stack([jnp.cos(angle), -jnp.sin(angle)], axis=0).astype(jnp.bfloat16)


def prep_kernel(spectra_ref, out_ref, theirs_ref, held_ref, sems, rows_ref):
    day = lax.axis_index("day")
    copies = []
    for which in range(2):
        half = (day + which) % 2
        copies.append(
            pltpu.make_async_copy(
                spectra_ref.at[pl.ds(half * 16, 16)],
                held_ref.at[pl.ds(which * 16, 16)],
                sems.at[which],
            )
        )
    for copy in copies:
        copy.start()
    low = lax.broadcasted_iota(jnp.int32, (BINS, 128), 1) < 64
    rows_ref[BINS * 16 :, :] = jnp.zeros(((SIDE * SHARE - BINS) * 16, 128), jnp.float32)
    for which in range(2):
        copies[which].wait()
        for pair in range(4):
            parts = []
            for a in (2 * pair, 2 * pair + 1):
                for q in range(2):
                    parts.append(held_ref[which * 16 + q * 8 + a].astype(jnp.float32))
            turned = jnp.concatenate(parts, axis=0).T
            re, im = turned[:BINS], turned[BINS:]
            power = re * re + im * im
            mean_power = jnp.mean(power, axis=0, keepdims=True)
            factor = lax.rsqrt(power + 0.25 * mean_power + 1e-06)
            re, im = re * factor, im * factor
            first = jnp.where(low, re, pltpu.roll(im, 64, 1))
            second = jnp.where(low, pltpu.roll(re, 64, 1), im)
            at = which * 8 + 2 * pair
            rows_ref[pl.ds(at, BINS, stride=16), :] = first
            rows_ref[pl.ds(at + 1, BINS, stride=16), :] = second
    for dest in range(SIDE):
        chunk = rows_ref[dest * ROWS : (dest + 1) * ROWS, :]
        out_ref[dest] = chunk.astype(jnp.bfloat16)
        theirs = chunk.reshape(SHARE, 2, 8, 128)[:, 1].reshape(HALF, 128)
        count = min(HALF, BINS * 8 - dest * HALF)
        if count > 0:
            theirs_ref[dest * HALF : dest * HALF + count, :] = theirs[:count].astype(jnp.bfloat16)


def prep(spectra):
    return pl.pallas_call(
        prep_kernel,
        out_shape=(
            jax.ShapeDtypeStruct((SIDE, ROWS, 128), jnp.bfloat16),
            jax.ShapeDtypeStruct((BINS * 8, 128), jnp.bfloat16),
        ),
        in_specs=[pl.BlockSpec(memory_space=pl.ANY)],
        out_specs=(VMEM, VMEM),
        scratch_shapes=[
            pltpu.VMEM(spectra.shape, jnp.bfloat16),
            pltpu.SemaphoreType.DMA((2,)),
            pltpu.VMEM((SIDE * ROWS, 128), jnp.float32),
        ],
        compiler_params=pltpu.CompilerParams(vmem_limit_bytes=60 * 1024 * 1024),
        name="prep",
    )(spectra)


def weights(value, day_of):
    swapped = jnp.concatenate([value[8:], value[:8]], axis=0)
    value = jnp.where(day_of == 0, value, swapped)
    lane = lax.broadcasted_iota(jnp.int32, value.shape, 1)
    odd = (lane // 32) % 2 == 1
    zero = jnp.zeros_like(value)
    even_v, odd_v = jnp.where(odd, zero, value), jnp.where(odd, value, zero)
    at = ((even_v, pltpu.roll(odd_v, 96, 1)), (pltpu.roll(even_v, 32, 1), odd_v))
    rows = []
    for q_i in range(2):
        for c in range(2):
            parts = []
            for q_j in range(2):
                part = at[q_i][q_j]
                if c == 1:
                    part = pltpu.roll(part, 64, 1)
                    part = jnp.where(lane < 64, -part, part)
                parts.append(part)
            rows.append(
                jnp.concatenate([parts[0][:8], parts[1][:8], parts[0][8:], parts[1][8:]], axis=0)
            )
    return rows


def cross_kernel(own_ref, other_ref, mine_ref, away_ref, out_ref):
    day = lax.axis_index("day")
    blocks = [
        [ref[step].astype(jnp.float32) for step in range(STEPS)] for ref in (mine_ref, away_ref)
    ]
    own_all = own_ref[...].astype(jnp.float32).reshape(SIDE, SHARE, 2, 8, 128)
    other_all = other_ref[...].astype(jnp.float32).reshape(SIDE, SHARE, 8, 128)
    for k in range(SHARE):
        sides = []
        for which in range(2):
            day_of = (day + which) % 2
            parts = [
                weights(blocks[which][step][k * 16 : k * 16 + 16], day_of) for step in range(STEPS)
            ]
            order = []
            for at in range(4):
                for step in range(STEPS):
                    order.append(parts[step][at])
            sides.append(jnp.concatenate(order, axis=0))
        right = jnp.concatenate(sides, axis=1).astype(jnp.bfloat16)
        own = own_all[:, k, 0].reshape(SIDE * 8, 128)
        other = other_all[:, k].reshape(SIDE * 8, 128)
        left = jnp.concatenate([own, other], axis=1).astype(jnp.bfloat16)
        product = lax.dot_general(
            left, right, (((1,), (1,)), ((), ())), preferred_element_type=jnp.float32
        )
        low = product[:, :128].reshape(SIDE, 8, 128)
        high = product[:, 128:].reshape(SIDE, 8, 128)
        both = jnp.concatenate([low, high], axis=1)
        out_ref[:, k * 16 : k * 16 + 16, :] = both.astype(jnp.bfloat16)


def cross(own, other, mine, away):
    return pl.pallas_call(
        cross_kernel,
        out_shape=jax.ShapeDtypeStruct((SIDE, ROWS, 128), jnp.bfloat16),
        in_specs=[VMEM] * 4,
        out_specs=VMEM,
        compiler_params=ROOM,
        name="cross",
    )(own, other, mine, away)


def lag_kernel(norm, summed_ref, table_ref, out_ref, rows_ref):
    rows_ref[...] = summed_ref[...].astype(jnp.float32).reshape(SIDE * ROWS, 128)
    for i in range(16):
        turned = rows_ref[pl.ds(i, BINS, stride=16), :].T.astype(jnp.bfloat16)
        lagged = jnp.dot(turned[:64], table_ref[0], preferred_element_type=jnp.float32)
        lagged = lagged + jnp.dot(turned[64:], table_ref[1], preferred_element_type=jnp.float32)
        lagged = (lagged * norm).astype(jnp.bfloat16)
        for step in range(STEPS):
            out_ref[step, i] = lagged[step * 32 : step * 32 + 32]


def lag(norm, summed, table):
    def kernel(*refs):
        lag_kernel(norm, *refs)

    return pl.pallas_call(
        kernel,
        out_shape=jax.ShapeDtypeStruct((STEPS, 16, 32, LAGS), jnp.bfloat16),
        in_specs=[VMEM, VMEM],
        out_specs=VMEM,
        scratch_shapes=[pltpu.VMEM((SIDE * ROWS, 128), jnp.float32)],
        compiler_params=ROOM,
        name="lag",
    )(summed, table)


def line(array, shift):
    return lax.ppermute(array, "z", [(at, (at + shift) % 4) for at in range(4)])


def swap(array):
    return lax.ppermute(array, "day", [(0, 1), (1, 0)])


def spread(array):
    return lax.all_to_all(array, PLANE, 0, 0, tiled=True)


def local(spectra, owners):
    z_lo = lax.axis_index("z")
    mine, theirs = prep(spectra)
    arrived = swap(theirs)
    own = spread(mine)
    pieces = []
    for step in range(STEPS):
        piece = lax.dynamic_index_in_dim(own, owners[step] % SIDE, 0, keepdims=False)
        pieces.append(jnp.where(owners[step] // SIDE == z_lo, piece, jnp.zeros_like(piece)))
    held = jnp.stack(pieces)
    block = held + line(held, 1) + line(held, 2) + line(held, 3)
    arrived = jnp.pad(arrived, ((0, SIDE * HALF - BINS * 8), (0, 0))).reshape(SIDE, HALF, 128)
    arrived, block = lax.optimization_barrier((arrived, block))
    other = spread(arrived)
    home = spread(cross(own, other, block, swap(block)))
    norm = 1.0 / math.sqrt(2 * spectra.shape[1] * BINS)
    return lag(norm, home, lag_table())


def solution(mesh):
    fine = Mesh(mesh.devices.reshape(4, 4, 4, 2, 2), ALL + ("day",))
    return jax.shard_map(
        local,
        mesh=fine,
        in_specs=(P(ALL, "day", None), P()),
        out_specs=P(None, ALL + ("day",), None, None),
        check_vma=False,
    )
```

```python
import math

import jax
import jax.numpy as jnp
from jax import lax
from jax.experimental import pallas as pl
from jax.experimental.pallas import tpu as pltpu
from jax.sharding import Mesh, PartitionSpec as P

LAGS = 400
STEPS = 2
BINS = 200
SHARE = 7
SIDE = 32
PLANE = ("x", "y", "core")
ALL = ("z", "x", "y", "core")
ROWS = SHARE * 16
HALF = SHARE * 8
VMEM = pl.BlockSpec(memory_space=pltpu.VMEM)
ROOM = pltpu.CompilerParams(vmem_limit_bytes=48 * 1024 * 1024)


def lag_table():
    freqs = jnp.arange(BINS, dtype=jnp.int32)
    shifts = jnp.arange(LAGS, dtype=jnp.int32) - LAGS // 2
    phase = jnp.mod(freqs[:, None] * shifts[None, :], 2 * BINS)
    angle = phase.astype(jnp.float32) * (math.pi / BINS)
    return jnp.stack([jnp.cos(angle), -jnp.sin(angle)], axis=0).astype(jnp.bfloat16)


def prep_kernel(spectra_ref, out_ref, theirs_ref, held_ref, sems, rows_ref):
    day = lax.axis_index("day")
    copies = []
    for which in range(2):
        half = (day + which) % 2
        copies.append(
            pltpu.make_async_copy(
                spectra_ref.at[pl.ds(half * 16, 16)],
                held_ref.at[pl.ds(which * 16, 16)],
                sems.at[which],
            )
        )
    for copy in copies:
        copy.start()
    low = lax.broadcasted_iota(jnp.int32, (BINS, 128), 1) < 64
    rows_ref[BINS * 16 :, :] = jnp.zeros(((SIDE * SHARE - BINS) * 16, 128), jnp.float32)
    for which in range(2):
        copies[which].wait()
        for pair in range(4):
            parts = []
            for a in (2 * pair, 2 * pair + 1):
                for q in range(2):
                    parts.append(held_ref[which * 16 + q * 8 + a].astype(jnp.float32))
            turned = jnp.concatenate(parts, axis=0).T
            re, im = turned[:BINS], turned[BINS:]
            power = re * re + im * im
            mean_power = jnp.mean(power, axis=0, keepdims=True)
            factor = lax.rsqrt(power + 0.25 * mean_power + 1e-06)
            re, im = re * factor, im * factor
            first = jnp.where(low, re, pltpu.roll(im, 64, 1))
            second = jnp.where(low, pltpu.roll(re, 64, 1), im)
            at = which * 8 + 2 * pair
            rows_ref[pl.ds(at, BINS, stride=16), :] = first
            rows_ref[pl.ds(at + 1, BINS, stride=16), :] = second
    for dest in range(SIDE):
        chunk = rows_ref[dest * ROWS : (dest + 1) * ROWS, :]
        out_ref[dest] = chunk.astype(jnp.bfloat16)
        theirs = chunk.reshape(SHARE, 2, 8, 128)[:, 1].reshape(HALF, 128)
        count = min(HALF, BINS * 8 - dest * HALF)
        if count > 0:
            theirs_ref[dest * HALF : dest * HALF + count, :] = theirs[:count].astype(jnp.bfloat16)


def prep(spectra):
    return pl.pallas_call(
        prep_kernel,
        out_shape=(
            jax.ShapeDtypeStruct((SIDE, ROWS, 128), jnp.bfloat16),
            jax.ShapeDtypeStruct((BINS * 8, 128), jnp.bfloat16),
        ),
        in_specs=[pl.BlockSpec(memory_space=pl.ANY)],
        out_specs=(VMEM, VMEM),
        scratch_shapes=[
            pltpu.VMEM(spectra.shape, jnp.bfloat16),
            pltpu.SemaphoreType.DMA((2,)),
            pltpu.VMEM((SIDE * ROWS, 128), jnp.float32),
        ],
        compiler_params=pltpu.CompilerParams(vmem_limit_bytes=60 * 1024 * 1024),
        name="prep",
    )(spectra)


def weights(value, day_of):
    swapped = jnp.concatenate([value[8:], value[:8]], axis=0)
    value = jnp.where(day_of == 0, value, swapped)
    lane = lax.broadcasted_iota(jnp.int32, value.shape, 1)
    odd = (lane // 32) % 2 == 1
    zero = jnp.zeros_like(value)
    even_v, odd_v = jnp.where(odd, zero, value), jnp.where(odd, value, zero)
    at = ((even_v, pltpu.roll(odd_v, 96, 1)), (pltpu.roll(even_v, 32, 1), odd_v))
    rows = []
    for q_i in range(2):
        for c in range(2):
            parts = []
            for q_j in range(2):
                part = at[q_i][q_j]
                if c == 1:
                    part = pltpu.roll(part, 64, 1)
                    part = jnp.where(lane < 64, -part, part)
                parts.append(part)
            rows.append(
                jnp.concatenate([parts[0][:8], parts[1][:8], parts[0][8:], parts[1][8:]], axis=0)
            )
    return rows


def cross_kernel(own_ref, other_ref, mine_ref, away_ref, out_ref):
    day = lax.axis_index("day")
    blocks = [
        [ref[step].astype(jnp.float32) for step in range(STEPS)] for ref in (mine_ref, away_ref)
    ]
    own_all = own_ref[...].astype(jnp.float32).reshape(SIDE, SHARE, 2, 8, 128)
    other_all = other_ref[...].astype(jnp.float32).reshape(SIDE, SHARE, 8, 128)
    for k in range(SHARE):
        sides = []
        for which in range(2):
            day_of = (day + which) % 2
            parts = [
                weights(blocks[which][step][k * 16 : k * 16 + 16], day_of) for step in range(STEPS)
            ]
            order = []
            for at in range(4):
                for step in range(STEPS):
                    order.append(parts[step][at])
            sides.append(jnp.concatenate(order, axis=0))
        right = jnp.concatenate(sides, axis=1).astype(jnp.bfloat16)
        own = own_all[:, k, 0].reshape(SIDE * 8, 128)
        other = other_all[:, k].reshape(SIDE * 8, 128)
        left = jnp.concatenate([own, other], axis=1).astype(jnp.bfloat16)
        product = lax.dot_general(
            left, right, (((1,), (1,)), ((), ())), preferred_element_type=jnp.float32
        )
        low = product[:, :128].reshape(SIDE, 8, 128)
        high = product[:, 128:].reshape(SIDE, 8, 128)
        both = jnp.concatenate([low, high], axis=1)
        out_ref[:, k * 16 : k * 16 + 16, :] = both.astype(jnp.bfloat16)


def cross(own, other, mine, away):
    return pl.pallas_call(
        cross_kernel,
        out_shape=jax.ShapeDtypeStruct((SIDE, ROWS, 128), jnp.bfloat16),
        in_specs=[VMEM] * 4,
        out_specs=VMEM,
        compiler_params=ROOM,
        name="cross",
    )(own, other, mine, away)


def lag_kernel(norm, summed_ref, table_ref, out_ref, rows_ref):
    rows_ref[...] = summed_ref[...].astype(jnp.float32).reshape(SIDE * ROWS, 128)
    for i in range(16):
        turned = rows_ref[pl.ds(i, BINS, stride=16), :].T.astype(jnp.bfloat16)
        lagged = jnp.dot(turned[:64], table_ref[0], preferred_element_type=jnp.float32)
        lagged = lagged + jnp.dot(turned[64:], table_ref[1], preferred_element_type=jnp.float32)
        lagged = (lagged * norm).astype(jnp.bfloat16)
        for step in range(STEPS):
            out_ref[step, i] = lagged[step * 32 : step * 32 + 32]


def lag(norm, summed, table):
    def kernel(*refs):
        lag_kernel(norm, *refs)

    return pl.pallas_call(
        kernel,
        out_shape=jax.ShapeDtypeStruct((STEPS, 16, 32, LAGS), jnp.bfloat16),
        in_specs=[VMEM, VMEM],
        out_specs=VMEM,
        scratch_shapes=[pltpu.VMEM((SIDE * ROWS, 128), jnp.float32)],
        compiler_params=ROOM,
        name="lag",
    )(summed, table)


def line(array, shift):
    return lax.ppermute(array, "z", [(at, at ^ shift) for at in range(4)])


def swap(array):
    return lax.ppermute(array, "day", [(0, 1), (1, 0)])


def spread(array):
    return lax.all_to_all(array, PLANE, 0, 0, tiled=True)


def local(spectra, owners):
    z_lo = lax.axis_index("z")
    mine, theirs = prep(spectra)
    arrived = swap(theirs)
    own = spread(mine)
    pieces = []
    for step in range(STEPS):
        piece = lax.dynamic_index_in_dim(own, owners[step] % SIDE, 0, keepdims=False)
        pieces.append(jnp.where(owners[step] // SIDE == z_lo, piece, jnp.zeros_like(piece)))
    held = jnp.stack(pieces)
    block = held + line(held, 1) + line(held, 2) + line(held, 3)
    arrived = jnp.pad(arrived, ((0, SIDE * HALF - BINS * 8), (0, 0))).reshape(SIDE, HALF, 128)
    arrived, block = lax.optimization_barrier((arrived, block))
    other = spread(arrived)
    home = spread(cross(own, other, block, swap(block)))
    norm = 1.0 / math.sqrt(2 * spectra.shape[1] * BINS)
    return lag(norm, home, lag_table())


def solution(mesh):
    fine = Mesh(mesh.devices.reshape(4, 4, 4, 2, 2), ALL + ("day",))
    return jax.shard_map(
        local,
        mesh=fine,
        in_specs=(P(ALL, "day", None), P()),
        out_specs=P(None, ALL + ("day",), None, None),
        check_vma=False,
    )
```

```python
import math

import jax
import jax.numpy as jnp
from jax import lax
from jax.experimental import pallas as pl
from jax.experimental.pallas import tpu as pltpu
from jax.sharding import Mesh, PartitionSpec as P

LAGS = 400
STEPS = 2
BINS = 200
SHARE = 7
SIDE = 32
PLANE = ("x", "y", "core")
ALL = ("z", "x", "y", "core")
ROWS = SHARE * 16
HALF = SHARE * 8
VMEM = pl.BlockSpec(memory_space=pltpu.VMEM)
ROOM = pltpu.CompilerParams(vmem_limit_bytes=48 * 1024 * 1024)


def lag_table():
    freqs = jnp.arange(BINS, dtype=jnp.int32)
    shifts = jnp.arange(LAGS, dtype=jnp.int32) - LAGS // 2
    phase = jnp.mod(freqs[:, None] * shifts[None, :], 2 * BINS)
    angle = phase.astype(jnp.float32) * (math.pi / BINS)
    return jnp.stack([jnp.cos(angle), -jnp.sin(angle)], axis=0).astype(jnp.bfloat16)


def prep_kernel(spectra_ref, out_ref, theirs_ref, held_ref, sems, rows_ref):
    day = lax.axis_index("day")
    copies = []
    for which in range(2):
        half = (day + which) % 2
        copies.append(
            pltpu.make_async_copy(
                spectra_ref.at[pl.ds(half * 16, 16)],
                held_ref.at[pl.ds(which * 16, 16)],
                sems.at[which],
            )
        )
    for copy in copies:
        copy.start()
    low = lax.broadcasted_iota(jnp.int32, (BINS, 128), 1) < 64
    rows_ref[BINS * 16 :, :] = jnp.zeros(((SIDE * SHARE - BINS) * 16, 128), jnp.float32)
    for which in range(2):
        copies[which].wait()
        for pair in range(4):
            parts = []
            for a in (2 * pair, 2 * pair + 1):
                for q in range(2):
                    parts.append(held_ref[which * 16 + q * 8 + a].astype(jnp.float32))
            turned = jnp.concatenate(parts, axis=0).T
            re, im = turned[:BINS], turned[BINS:]
            power = re * re + im * im
            mean_power = jnp.mean(power, axis=0, keepdims=True)
            factor = lax.rsqrt(power + 0.25 * mean_power + 1e-06)
            re, im = re * factor, im * factor
            first = jnp.where(low, re, pltpu.roll(im, 64, 1))
            second = jnp.where(low, pltpu.roll(re, 64, 1), im)
            at = which * 8 + 2 * pair
            rows_ref[pl.ds(at, BINS, stride=16), :] = first
            rows_ref[pl.ds(at + 1, BINS, stride=16), :] = second
    for dest in range(SIDE):
        chunk = rows_ref[dest * ROWS : (dest + 1) * ROWS, :]
        out_ref[dest] = chunk.astype(jnp.bfloat16)
        theirs = chunk.reshape(SHARE, 2, 8, 128)[:, 1].reshape(HALF, 128)
        count = min(HALF, BINS * 8 - dest * HALF)
        if count > 0:
            theirs_ref[dest * HALF : dest * HALF + count, :] = theirs[:count].astype(jnp.bfloat16)


def prep(spectra):
    return pl.pallas_call(
        prep_kernel,
        out_shape=(
            jax.ShapeDtypeStruct((SIDE, ROWS, 128), jnp.bfloat16),
            jax.ShapeDtypeStruct((BINS * 8, 128), jnp.bfloat16),
        ),
        in_specs=[pl.BlockSpec(memory_space=pl.ANY)],
        out_specs=(VMEM, VMEM),
        scratch_shapes=[
            pltpu.VMEM(spectra.shape, jnp.bfloat16),
            pltpu.SemaphoreType.DMA((2,)),
            pltpu.VMEM((SIDE * ROWS, 128), jnp.float32),
        ],
        compiler_params=pltpu.CompilerParams(vmem_limit_bytes=60 * 1024 * 1024),
        name="prep",
    )(spectra)


def weights(value, day_of):
    swapped = jnp.concatenate([value[8:], value[:8]], axis=0)
    value = jnp.where(day_of == 0, value, swapped)
    lane = lax.broadcasted_iota(jnp.int32, value.shape, 1)
    odd = (lane // 32) % 2 == 1
    zero = jnp.zeros_like(value)
    even_v, odd_v = jnp.where(odd, zero, value), jnp.where(odd, value, zero)
    at = ((even_v, pltpu.roll(odd_v, 96, 1)), (pltpu.roll(even_v, 32, 1), odd_v))
    rows = []
    for q_i in range(2):
        for c in range(2):
            parts = []
            for q_j in range(2):
                part = at[q_i][q_j]
                if c == 1:
                    part = pltpu.roll(part, 64, 1)
                    part = jnp.where(lane < 64, -part, part)
                parts.append(part)
            rows.append(
                jnp.concatenate([parts[0][:8], parts[1][:8], parts[0][8:], parts[1][8:]], axis=0)
            )
    return rows


def cross_kernel(own_ref, other_ref, mine_ref, away_ref, out_ref):
    day = lax.axis_index("day")
    blocks = [
        [ref[step].astype(jnp.float32) for step in range(STEPS)] for ref in (mine_ref, away_ref)
    ]
    own_all = own_ref[...].astype(jnp.float32).reshape(SIDE, SHARE, 2, 8, 128)
    other_all = other_ref[...].astype(jnp.float32).reshape(SIDE, SHARE, 8, 128)
    for k in range(SHARE):
        sides = []
        for which in range(2):
            day_of = (day + which) % 2
            parts = [
                weights(blocks[which][step][k * 16 : k * 16 + 16], day_of) for step in range(STEPS)
            ]
            order = []
            for at in range(4):
                for step in range(STEPS):
                    order.append(parts[step][at])
            sides.append(jnp.concatenate(order, axis=0))
        right = jnp.concatenate(sides, axis=1).astype(jnp.bfloat16)
        own = own_all[:, k, 0].reshape(SIDE * 8, 128)
        other = other_all[:, k].reshape(SIDE * 8, 128)
        left = jnp.concatenate([own, other], axis=1).astype(jnp.bfloat16)
        product = lax.dot_general(
            left, right, (((1,), (1,)), ((), ())), preferred_element_type=jnp.float32
        )
        low = product[:, :128].reshape(SIDE, 8, 128)
        high = product[:, 128:].reshape(SIDE, 8, 128)
        both = jnp.concatenate([low, high], axis=1)
        out_ref[:, k * 16 : k * 16 + 16, :] = both.astype(jnp.bfloat16)


def cross(own, other, mine, away):
    return pl.pallas_call(
        cross_kernel,
        out_shape=jax.ShapeDtypeStruct((SIDE, ROWS, 128), jnp.bfloat16),
        in_specs=[VMEM] * 4,
        out_specs=VMEM,
        compiler_params=ROOM,
        name="cross",
    )(own, other, mine, away)


def lag_kernel(norm, summed_ref, table_ref, out_ref, rows_ref):
    rows_ref[...] = summed_ref[...].astype(jnp.float32).reshape(SIDE * ROWS, 128)
    for i in range(16):
        turned = rows_ref[pl.ds(i, BINS, stride=16), :].T.astype(jnp.bfloat16)
        lagged = jnp.dot(turned[:64], table_ref[0], preferred_element_type=jnp.float32)
        lagged = lagged + jnp.dot(turned[64:], table_ref[1], preferred_element_type=jnp.float32)
        lagged = (lagged * norm).astype(jnp.bfloat16)
        for step in range(STEPS):
            out_ref[step, i] = lagged[step * 32 : step * 32 + 32]


def lag(norm, summed, table):
    def kernel(*refs):
        lag_kernel(norm, *refs)

    return pl.pallas_call(
        kernel,
        out_shape=jax.ShapeDtypeStruct((STEPS, 16, 32, LAGS), jnp.bfloat16),
        in_specs=[VMEM, VMEM],
        out_specs=VMEM,
        scratch_shapes=[pltpu.VMEM((SIDE * ROWS, 128), jnp.float32)],
        compiler_params=ROOM,
        name="lag",
    )(summed, table)


def pad_kernel(in_ref, out_ref):
    out_ref[: BINS * 8, :] = in_ref[...]
    out_ref[BINS * 8 :, :] = jnp.zeros((SIDE * HALF - BINS * 8, 128), jnp.bfloat16)


def pad(array):
    return pl.pallas_call(
        pad_kernel,
        out_shape=jax.ShapeDtypeStruct((SIDE * HALF, 128), jnp.bfloat16),
        in_specs=[VMEM],
        out_specs=VMEM,
        name="pad",
    )(array).reshape(SIDE, HALF, 128)


def line(array, shift):
    return lax.ppermute(array, "z", [(at, at ^ shift) for at in range(4)])


def swap(array):
    return lax.ppermute(array, "day", [(0, 1), (1, 0)])


def spread(array):
    return lax.all_to_all(array, PLANE, 0, 0, tiled=True)


def local(spectra, owners):
    z_lo = lax.axis_index("z")
    mine, theirs = prep(spectra)
    arrived = swap(theirs)
    own = spread(mine)
    pieces = []
    for step in range(STEPS):
        piece = lax.dynamic_index_in_dim(own, owners[step] % SIDE, 0, keepdims=False)
        pieces.append(jnp.where(owners[step] // SIDE == z_lo, piece, jnp.zeros_like(piece)))
    held = jnp.stack(pieces)
    block = held + line(held, 1) + line(held, 2) + line(held, 3)
    arrived = pad(arrived)
    arrived, block = lax.optimization_barrier((arrived, block))
    other = spread(arrived)
    home = spread(cross(own, other, block, swap(block)))
    norm = 1.0 / math.sqrt(2 * spectra.shape[1] * BINS)
    return lag(norm, home, lag_table())


def solution(mesh):
    fine = Mesh(mesh.devices.reshape(4, 4, 4, 2, 2), ALL + ("day",))
    return jax.shard_map(
        local,
        mesh=fine,
        in_specs=(P(ALL, "day", None), P()),
        out_specs=P(None, ALL + ("day",), None, None),
        check_vma=False,
    )
```

```python
import math

import jax
import jax.numpy as jnp
from jax import lax
from jax.experimental import pallas as pl
from jax.experimental.pallas import tpu as pltpu
from jax.sharding import Mesh, PartitionSpec as P

LAGS = 400
STEPS = 2
BINS = 200
SHARE = 7
SIDE = 32
PLANE = ("x", "y", "core")
ALL = ("z", "x", "y", "core")
ROWS = SHARE * 16
HALF = SHARE * 8
VMEM = pl.BlockSpec(memory_space=pltpu.VMEM)
ROOM = pltpu.CompilerParams(vmem_limit_bytes=48 * 1024 * 1024)


def lag_table():
    freqs = jnp.arange(BINS, dtype=jnp.int32)
    shifts = jnp.arange(LAGS, dtype=jnp.int32) - LAGS // 2
    phase = jnp.mod(freqs[:, None] * shifts[None, :], 2 * BINS)
    angle = phase.astype(jnp.float32) * (math.pi / BINS)
    return jnp.stack([jnp.cos(angle), -jnp.sin(angle)], axis=0).astype(jnp.bfloat16)


def prep_kernel(spectra_ref, out_ref, theirs_ref, held_ref, sems, rows_ref):
    day = lax.axis_index("day")
    copies = []
    for which in range(2):
        half = (day + which) % 2
        copies.append(
            pltpu.make_async_copy(
                spectra_ref.at[pl.ds(half * 16, 16)],
                held_ref.at[pl.ds(which * 16, 16)],
                sems.at[which],
            )
        )
    for copy in copies:
        copy.start()
    low = lax.broadcasted_iota(jnp.int32, (BINS, 128), 1) < 64
    rows_ref[BINS * 16 :, :] = jnp.zeros(((SIDE * SHARE - BINS) * 16, 128), jnp.float32)
    for which in range(2):
        copies[which].wait()
        for pair in range(4):
            parts = []
            for a in (2 * pair, 2 * pair + 1):
                for q in range(2):
                    parts.append(held_ref[which * 16 + q * 8 + a].astype(jnp.float32))
            turned = jnp.concatenate(parts, axis=0).T
            re, im = turned[:BINS], turned[BINS:]
            power = re * re + im * im
            mean_power = jnp.mean(power, axis=0, keepdims=True)
            factor = lax.rsqrt(power + 0.25 * mean_power + 1e-06)
            re, im = re * factor, im * factor
            first = jnp.where(low, re, pltpu.roll(im, 64, 1))
            second = jnp.where(low, pltpu.roll(re, 64, 1), im)
            at = which * 8 + 2 * pair
            rows_ref[pl.ds(at, BINS, stride=16), :] = first
            rows_ref[pl.ds(at + 1, BINS, stride=16), :] = second
    for dest in range(SIDE):
        chunk = rows_ref[dest * ROWS : (dest + 1) * ROWS, :]
        out_ref[dest] = chunk.astype(jnp.bfloat16)
        theirs = chunk.reshape(SHARE, 2, 8, 128)[:, 1].reshape(HALF, 128)
        count = min(HALF, BINS * 8 - dest * HALF)
        if count > 0:
            theirs_ref[dest * HALF : dest * HALF + count, :] = theirs[:count].astype(jnp.bfloat16)


def prep(spectra):
    return pl.pallas_call(
        prep_kernel,
        out_shape=(
            jax.ShapeDtypeStruct((SIDE, ROWS, 128), jnp.bfloat16),
            jax.ShapeDtypeStruct((BINS * 8, 128), jnp.bfloat16),
        ),
        in_specs=[pl.BlockSpec(memory_space=pl.ANY)],
        out_specs=(VMEM, VMEM),
        scratch_shapes=[
            pltpu.VMEM(spectra.shape, jnp.bfloat16),
            pltpu.SemaphoreType.DMA((2,)),
            pltpu.VMEM((SIDE * ROWS, 128), jnp.float32),
        ],
        compiler_params=pltpu.CompilerParams(vmem_limit_bytes=60 * 1024 * 1024),
        name="prep",
    )(spectra)


def weights(value, day_of):
    swapped = jnp.concatenate([value[8:], value[:8]], axis=0)
    value = jnp.where(day_of == 0, value, swapped)
    lane = lax.broadcasted_iota(jnp.int32, value.shape, 1)
    odd = (lane // 32) % 2 == 1
    zero = jnp.zeros_like(value)
    even_v, odd_v = jnp.where(odd, zero, value), jnp.where(odd, value, zero)
    at = ((even_v, pltpu.roll(odd_v, 96, 1)), (pltpu.roll(even_v, 32, 1), odd_v))
    rows = []
    for q_i in range(2):
        for c in range(2):
            parts = []
            for q_j in range(2):
                part = at[q_i][q_j]
                if c == 1:
                    part = pltpu.roll(part, 64, 1)
                    part = jnp.where(lane < 64, -part, part)
                parts.append(part)
            rows.append(
                jnp.concatenate([parts[0][:8], parts[1][:8], parts[0][8:], parts[1][8:]], axis=0)
            )
    return rows


def cross_kernel(own_ref, other_ref, mine_ref, away_ref, out_ref):
    day = lax.axis_index("day")
    blocks = [
        [ref[step].astype(jnp.float32) for step in range(STEPS)] for ref in (mine_ref, away_ref)
    ]
    own_all = own_ref[...].astype(jnp.float32).reshape(SIDE, SHARE, 2, 8, 128)
    other_all = other_ref[...].astype(jnp.float32).reshape(SIDE, SHARE, 8, 128)
    for k in range(SHARE):
        sides = []
        for which in range(2):
            day_of = (day + which) % 2
            parts = [
                weights(blocks[which][step][k * 16 : k * 16 + 16], day_of) for step in range(STEPS)
            ]
            order = []
            for at in range(4):
                for step in range(STEPS):
                    order.append(parts[step][at])
            sides.append(jnp.concatenate(order, axis=0))
        right = jnp.concatenate(sides, axis=1).astype(jnp.bfloat16)
        own = own_all[:, k, 0].reshape(SIDE * 8, 128)
        other = other_all[:, k].reshape(SIDE * 8, 128)
        left = jnp.concatenate([own, other], axis=1).astype(jnp.bfloat16)
        product = lax.dot_general(
            left, right, (((1,), (1,)), ((), ())), preferred_element_type=jnp.float32
        )
        low = product[:, :128].reshape(SIDE, 8, 128)
        high = product[:, 128:].reshape(SIDE, 8, 128)
        both = jnp.concatenate([low, high], axis=1)
        out_ref[:, k * 16 : k * 16 + 16, :] = both.astype(jnp.bfloat16)


def cross(own, other, mine, away):
    return pl.pallas_call(
        cross_kernel,
        out_shape=jax.ShapeDtypeStruct((SIDE, ROWS, 128), jnp.bfloat16),
        in_specs=[VMEM] * 4,
        out_specs=VMEM,
        compiler_params=ROOM,
        name="cross",
    )(own, other, mine, away)


def lag_kernel(norm, summed_ref, table_ref, out_ref, rows_ref, held_ref, sems):
    started = []
    rows_ref[...] = summed_ref[...].astype(jnp.float32).reshape(SIDE * ROWS, 128)
    for i in range(16):
        turned = rows_ref[pl.ds(i, BINS, stride=16), :].T.astype(jnp.bfloat16)
        lagged = jnp.dot(turned[:64], table_ref[0], preferred_element_type=jnp.float32)
        lagged = lagged + jnp.dot(turned[64:], table_ref[1], preferred_element_type=jnp.float32)
        lagged = (lagged * norm).astype(jnp.bfloat16)
        for step in range(STEPS):
            held_ref[step, i] = lagged[step * 32 : step * 32 + 32]
        if i % 4 == 3:
            for step in range(STEPS):
                part = pl.ds(i - 3, 4)
                copy = pltpu.make_async_copy(
                    held_ref.at[step, part], out_ref.at[step, part], sems.at[i // 4 * 2 + step]
                )
                copy.start()
                started.append(copy)
    for copy in started:
        copy.wait()


def lag(norm, summed, table):
    def kernel(*refs):
        lag_kernel(norm, *refs)

    return pl.pallas_call(
        kernel,
        out_shape=jax.ShapeDtypeStruct((STEPS, 16, 32, LAGS), jnp.bfloat16),
        in_specs=[VMEM, VMEM],
        out_specs=pl.BlockSpec(memory_space=pl.ANY),
        scratch_shapes=[
            pltpu.VMEM((SIDE * ROWS, 128), jnp.float32),
            pltpu.VMEM((STEPS, 16, 32, LAGS), jnp.bfloat16),
            pltpu.SemaphoreType.DMA((8,)),
        ],
        compiler_params=ROOM,
        name="lag",
    )(summed, table)


def line(array, shift):
    return lax.ppermute(array, "z", [(at, at ^ shift) for at in range(4)])


def swap(array):
    return lax.ppermute(array, "day", [(0, 1), (1, 0)])


def spread(array):
    return lax.all_to_all(array, PLANE, 0, 0, tiled=True)


def local(spectra, owners):
    z_lo = lax.axis_index("z")
    mine, theirs = prep(spectra)
    arrived = swap(theirs)
    own = spread(mine)
    pieces = []
    for step in range(STEPS):
        piece = lax.dynamic_index_in_dim(own, owners[step] % SIDE, 0, keepdims=False)
        pieces.append(jnp.where(owners[step] // SIDE == z_lo, piece, jnp.zeros_like(piece)))
    held = jnp.stack(pieces)
    block = held + line(held, 1) + line(held, 2) + line(held, 3)
    arrived = jnp.pad(arrived, ((0, SIDE * HALF - BINS * 8), (0, 0))).reshape(SIDE, HALF, 128)
    arrived, block = lax.optimization_barrier((arrived, block))
    other = spread(arrived)
    home = spread(cross(own, other, block, swap(block)))
    norm = 1.0 / math.sqrt(2 * spectra.shape[1] * BINS)
    return lag(norm, home, lag_table())


def solution(mesh):
    fine = Mesh(mesh.devices.reshape(4, 4, 4, 2, 2), ALL + ("day",))
    return jax.shard_map(
        local,
        mesh=fine,
        in_specs=(P(ALL, "day", None), P()),
        out_specs=P(None, ALL + ("day",), None, None),
        check_vma=False,
    )
```
